32 devices in a mesh: groups: 2 (over y), dp: 4 (over z), tensor: 4 (over x, core).
Axes of the slice: x: 2, y: 2, z: 4, core: 2. Of those that a mesh axis runs over, the one named last changes fastest.
Arguments:
- residual: bfloat16 [8192, 3072], P(('groups', 'dp'), 'tensor'), parts along dimension 0, may hold values from -6 to 6
- attention: bfloat16 [8192, 3072], P(('groups', 'dp'), 'tensor'), parts along dimension 0, may hold values from -6 to 6
- gate: bfloat16 [128, 3072], P(('groups', 'dp'), 'tensor'), parts along dimension 0, may hold values from 0.5 to 1.5
- output_projection_weight: bfloat16 [3072, 3072], P(None, 'tensor'), may hold values from -0.109375 to 0.109375
- adapter_down_weight: bfloat16 [32, 64, 3072], P('dp', None, 'tensor'), may hold values from -0.109375 to 0.109375
- adapter_up_weight: bfloat16 [32, 64, 3072], P('dp', None, 'tensor'), may hold values from -0.75 to 0.75
- request_adapter_index: int32 [128], P(('groups', 'dp')), parts along dimension 0, may hold values from 0 to 31, as said below
Outputs:
- updated: bfloat16 [8192, 3072], P(('groups', 'dp'), 'tensor'), parts along dimension 0
The draws below stay inside these ranges and needn't reach their ends.
There are 2 independent parts, one for each index of `groups`. The reference program is written for one: setup_inputs(seed, part) draws one part's arguments, and reference() takes and returns one part's arrays. A program takes and returns all parts, laid end to end along the dimension named above; an argument that names none is the same for every part. Nothing has to cross between parts.
Inputs may be any that keep to these rules, and one draw needn't show every extreme that they name: `request_adapter_index`: at most 8 of the requests of one index of dp use adapters held by one index of dp; in every draw one index of dp holds the adapters of exactly 8 requests of every index of dp.
All inputs are finite; a program needn't handle non-finite values.
Results may differ from the reference program's by a relative error of at most 0.0043.
Values may be sent and summed in bfloat16 or wider, within the bound.
A program may use at most 128 MiB of HBM per device.

```python
import jax
import jax.numpy as jnp
from jax import lax

MODEL_WIDTH = 3072
ADAPTER_RANK = 64
WIN = 64
REQ_DEV = 16
ADP_DEV = 8
REQUESTS = 64
ROWS = 4096
ADAPTER_COUNT = 32
CAP = 8


def draw_request_adapter_index(key, part):
    key = jax.random.fold_in(key, 11)
    holders = REQUESTS // REQ_DEV
    key_hot, key_rest, key_order, key_local = jax.random.split(key, 4)
    hottest = jax.random.randint(key_hot, (), 0, holders)
    rest_keys = jax.random.split(key_rest, holders)
    rest = jax.vmap(lambda k: jax.random.permutation(k, (holders - 1) * CAP))(rest_keys)
    rest = rest[:, :REQ_DEV - CAP]
    rest_owner = (hottest + 1 + rest // CAP) % holders
    owners = jnp.concatenate([jnp.full((holders, CAP), hottest, jnp.int32), rest_owner.astype(jnp.int32)], axis=1)
    order_keys = jax.random.split(key_order, holders)
    order = jax.vmap(lambda k: jax.random.permutation(k, REQ_DEV))(order_keys)
    owners = jnp.take_along_axis(owners, order, axis=1)
    local = jax.random.randint(key_local, (holders, REQ_DEV), 0, ADP_DEV)
    return (owners * ADP_DEV + local).reshape(-1).astype(jnp.int32)


def steps_of(rng, extent, cuts, low, top_value):
    def one(dim, parts):
        steps = jax.random.uniform(jax.random.fold_in(jax.random.fold_in(rng, 6), dim), (parts,), jnp.float32, low / len(cuts), top_value / len(cuts))
        return jnp.repeat(jnp.exp(steps), extent[dim] // parts).reshape((-1,) + (1,) * (len(extent) - dim - 1))

    level = one(*cuts[0])
    for cut in cuts[1:]:
        level = level * one(*cut)
    return level


def gaussian(key, extent, deviation, limit, pieces=(), dtype=jnp.bfloat16):
    array = jax.random.normal(key, extent, jnp.float32) * deviation
    if len(pieces) > 0:
        array = steps_of(key, extent, pieces, -0.22, 0.18) * array
    return jnp.clip(array, min=-limit, max=limit).astype(dtype)


def setup_inputs(seed: int = 0, part: int = 0) -> dict:
    splits = jax.random.split(jax.random.key(seed), 8)
    part_keys = jax.random.split(jax.random.fold_in(splits[7], part), 8)
    residual = gaussian(part_keys[0], (ROWS, MODEL_WIDTH), 1.0, 6.0, ((0, 4), (1, 4)))
    attention = gaussian(part_keys[1], (ROWS, MODEL_WIDTH), 1.0, 6.0, ((0, 4), (1, 4)))
    gate = jnp.clip(0.5 + 1.0 * jax.random.uniform(part_keys[2], (REQUESTS, MODEL_WIDTH), jnp.float32) ** steps_of(part_keys[2], (REQUESTS, MODEL_WIDTH), ((0, 4), (1, 4)), -0.2, 0.2), 0.5, 1.5).astype(jnp.bfloat16)
    output_projection_weight = gaussian(splits[3], (MODEL_WIDTH, MODEL_WIDTH), MODEL_WIDTH ** -0.5, 0.109375, ((1, 4),))
    adapter_down_weight = gaussian(splits[4], (ADAPTER_COUNT, ADAPTER_RANK, MODEL_WIDTH), MODEL_WIDTH ** -0.5, 0.109375, ((0, 4), (2, 4)))
    adapter_up_weight = gaussian(splits[5], (ADAPTER_COUNT, ADAPTER_RANK, MODEL_WIDTH), ADAPTER_RANK ** -0.5, 0.75, ((0, 4), (2, 4)))
    request_adapter_index = draw_request_adapter_index(jax.random.fold_in(jax.random.fold_in(splits[7], part), 71), part)
    return dict(residual=residual, attention=attention, gate=gate, output_projection_weight=output_projection_weight, adapter_down_weight=adapter_down_weight, adapter_up_weight=adapter_up_weight, request_adapter_index=request_adapter_index)


def reference(residual, attention, gate, output_projection_weight, adapter_down_weight, adapter_up_weight, request_adapter_index):
    base = jnp.dot(attention, output_projection_weight, preferred_element_type=jnp.float32)
    blocks = attention.reshape(REQUESTS, WIN, MODEL_WIDTH)

    def one_request(item):
        rows, selected_adapter = item
        down_matrix = lax.dynamic_index_in_dim(adapter_down_weight, selected_adapter.astype(jnp.int32), 0, keepdims=False)
        up_matrix = lax.dynamic_index_in_dim(adapter_up_weight, selected_adapter.astype(jnp.int32), 0, keepdims=False)
        low = jnp.dot(rows, down_matrix.T, preferred_element_type=jnp.float32).astype(jnp.bfloat16)
        return jnp.dot(low, up_matrix, preferred_element_type=jnp.float32).astype(jnp.bfloat16)

    delta = lax.map(one_request, (blocks, request_adapter_index)).reshape(ROWS, MODEL_WIDTH)
    delta = lax.optimization_barrier(delta).astype(jnp.float32)
    scale = jnp.repeat(gate, WIN, axis=0).astype(jnp.float32)
    updated = residual.astype(jnp.float32) + scale * (base + delta)
    return updated.astype(jnp.bfloat16)
```

```python
import functools

import jax
import jax.numpy as jnp
from jax import lax
from jax.experimental import pallas as pl
from jax.experimental.pallas import tpu as pltpu
from jax.sharding import PartitionSpec as P

MESH = pl.DeviceIdType.MESH
PIECES = 2
PARTS = 4


def exchange_body(
    residual,
    attention,
    gate,
    output_projection_weight,
    adapter_down_weight,
    adapter_up_weight,
    request_adapter_index,
):
    rows, width = attention.shape
    req_dev = request_adapter_index.shape[0]
    window = rows // req_dev
    holders = lax.axis_size("dp")
    adapter_device_share = adapter_down_weight.shape[0]
    capacity = max(1, 2 * req_dev // holders)
    total = holders * capacity
    owner = request_adapter_index // adapter_device_share
    local = request_adapter_index % adapter_device_share
    same_owner = owner[:, None] == owner[None, :]
    earlier = jnp.arange(req_dev)[None, :] < jnp.arange(req_dev)[:, None]
    place = jnp.sum(jnp.logical_and(same_owner, earlier).astype(jnp.int32), axis=1)
    target = owner * capacity + place
    onehot = jnp.arange(total)[:, None] == target[None, :]
    chosen = onehot.astype(jnp.bfloat16)
    flat = attention.reshape(req_dev, window * width)
    packed = jnp.dot(chosen, flat, preferred_element_type=jnp.float32).astype(jnp.bfloat16)
    packed = packed.reshape(holders, capacity, window, width)
    wanted = jnp.sum(onehot.astype(jnp.int32) * local[None, :], axis=1)
    wanted = wanted.reshape(holders, capacity)
    got_rows = lax.all_to_all(packed, "dp", split_axis=0, concat_axis=0, tiled=True)
    received_slots = lax.all_to_all(wanted, "dp", split_axis=0, concat_axis=0, tiled=True)
    down_matrix = jnp.take(adapter_down_weight, received_slots, axis=0)
    up_matrix = jnp.take(adapter_up_weight, received_slots, axis=0)
    partial_low = jnp.einsum(
        "ncwf,ncrf->ncwr", got_rows, down_matrix, preferred_element_type=jnp.float32
    )
    array_shape = partial_low.shape
    summed = lax.psum(
        partial_low.reshape(array_shape[0], array_shape[1], array_shape[2] * array_shape[3]),
        "tensor",
    )
    low = summed.reshape(array_shape).astype(jnp.bfloat16)
    delta = jnp.einsum(
        "ncwr,ncrf->ncwf", low, up_matrix, preferred_element_type=jnp.float32
    ).astype(jnp.bfloat16)
    returned = lax.all_to_all(delta, "dp", split_axis=0, concat_axis=0, tiled=True)
    gathered_back = jnp.dot(
        chosen.T, returned.reshape(total, window * width), preferred_element_type=jnp.float32
    )
    delta_rows = gathered_back.reshape(rows, width)
    base = jnp.dot(
        lax.all_gather(attention, "tensor", axis=1, tiled=True),
        output_projection_weight,
        preferred_element_type=jnp.float32,
    )
    scale = jnp.repeat(gate, window, axis=0).astype(jnp.float32)
    updated = residual.astype(jnp.float32) + scale * (base + delta_rows)
    return updated.astype(jnp.bfloat16)


def fused_kernel(
    holders,
    index,
    gate_in,
    residual_in,
    attention_in,
    weight_in,
    down_in,
    up_in,
    out,
    attention,
    weight,
    down,
    up,
    residual,
    gate,
    total,
    result,
    partial,
    arrived,
    low,
    z_send,
    z_recv,
    y_send,
    y_recv,
    x_send,
    x_recv,
    near_send,
    near_recv,
    pass_send,
    pass_recv,
    sum_send,
    sum_recv,
    low_send,
    low_recv,
    local_sem,
    out_sem,
):
    g = lax.axis_index("groups")
    d = lax.axis_index("dp")
    t = lax.axis_index("tensor")
    core = lax.rem(t, 2)
    sibling = t + 1 - 2 * core
    across = lax.rem(t + 2, 4)
    diagonal = lax.rem(sibling + 2, 4)

    rows, width = attention_in.shape
    requests = gate_in.shape[0]
    window = rows // requests
    share, rank, _ = down_in.shape
    half = share // 2
    piece = half // PIECES
    part_rows = rows // PARTS
    pairs = requests // 2
    own_pairs = pairs // 4
    hops = holders - 1
    inputs, buffers = (down_in, up_in), (down, up)

    own_block = pl.ds(d * share, share)
    local = [
        pltpu.make_async_copy(src, dst, local_sem.at[i])
        for i, (src, dst) in enumerate(
            [
                (attention_in, attention.at[t]),
                (down_in, down.at[own_block]),
                (weight_in, weight),
                (residual_in, residual),
                (up_in, up.at[own_block]),
            ]
        )
    ]

    barrier = pltpu.get_barrier_semaphore()

    def greet(where):
        pl.semaphore_signal(barrier, inc=1, device_id=where, device_id_type=MESH)

    for step in (1, 2, 3):
        greet({"tensor": lax.rem(t + step, 4)})
    greet({"groups": 1 - g})

    @pl.when(d > 0)
    def _():
        greet({"dp": d - 1})

    @pl.when(d < holders - 1)
    def _():
        greet({"dp": d + 1})

    for copy in local:
        copy.start()
    pl.semaphore_wait(barrier, 4 + (d > 0).astype(jnp.int32) + (d < holders - 1).astype(jnp.int32))

    def slot(stage, way, hop, j):
        return ((stage * 2 + way) * hops + hop) * PIECES + j

    def place(holder, side, j):
        return pl.ds(holder * share + side * half + j * piece, piece)

    def rank_on(way):
        return d if way == 0 else holders - 1 - d

    def sends(way, hop):
        e = rank_on(way)
        return jnp.logical_and(e < holders - 1, e >= hop)

    def receives(way, hop):
        return rank_on(way) > hop

    def z_copy(stage, way, hop, j):
        sign = 1 if way == 0 else -1
        target = buffers[stage].at[place(d - sign * hop, g, j)]
        source = inputs[stage].at[pl.ds(g * half + j * piece, piece)] if hop == 0 else target
        i = slot(stage, way, hop, j)
        return pltpu.make_async_remote_copy(
            src_ref=source, dst_ref=target, send_sem=z_send.at[i], recv_sem=z_recv.at[i],
            device_id={"dp": d + sign}, device_id_type=MESH,
        )

    def z_arrival(stage, way, hop, j):
        sign = 1 if way == 0 else -1
        target = buffers[stage].at[place(d - sign * (hop + 1), g, j)]
        i = slot(stage, way, hop, j)
        return pltpu.make_async_remote_copy(
            src_ref=target, dst_ref=target, send_sem=z_send.at[i], recv_sem=z_recv.at[i],
            device_id={"dp": d - sign}, device_id_type=MESH,
        )

    def y_copy(stage, way, hop, j, side):
        sign = 1 if way == 0 else -1
        target = buffers[stage].at[place(d - sign * (hop + 1), side, j)]
        i = slot(stage, way, hop, j)
        return pltpu.make_async_remote_copy(
            src_ref=target, dst_ref=target, send_sem=y_send.at[i], recv_sem=y_recv.at[i],
            device_id={"groups": 1 - g}, device_id_type=MESH,
        )

    def start_own(stage):
        for j in range(PIECES):
            for way in (0, 1):
                @pl.when(sends(way, 0))
                def _():
                    z_copy(stage, way, 0, j).start()

    def relay(stage, hop, j):
        for way in (0, 1):
            @pl.when(receives(way, hop))
            def _():
                z_arrival(stage, way, hop, j).wait_recv()
                if hop + 1 < hops:
                    @pl.when(sends(way, hop + 1))
                    def _():
                        z_copy(stage, way, hop + 1, j).start()
                y_copy(stage, way, hop, j, g).start()

    def await_other_group(stage):
        for hop in range(hops):
            for j in range(PIECES):
                for way in (0, 1):
                    @pl.when(receives(way, hop))
                    def _():
                        y_copy(stage, way, hop, j, 1 - g).wait_recv()

    def part(q):
        return pl.ds(q * part_rows, part_rows)

    def attention_copy(source, which, q, send, recv, to):
        return pltpu.make_async_remote_copy(
            src_ref=source, dst_ref=attention.at[which, part(q)],
            send_sem=send.at[q], recv_sem=recv.at[q],
            device_id={"tensor": to}, device_id_type=MESH,
        )

    def across_copy(q):
        return attention_copy(attention_in.at[part(q)], t, q, x_send, x_recv, across)

    def near_copy(q):
        return attention_copy(attention_in.at[part(q)], t, q, near_send, near_recv, sibling)

    def pass_copy(q):
        return attention_copy(attention.at[across, part(q)], across, q, pass_send, pass_recv, sibling)

    def relay_attention(q):
        attention_copy(attention.at[across, part(q)], across, q, x_send, x_recv, across).wait_recv()
        pass_copy(q).start()

    tile = 256

    def base_part(q):
        attention_copy(attention.at[sibling, part(q)], sibling, q, near_send, near_recv, sibling).wait_recv()
        attention_copy(attention.at[diagonal, part(q)], diagonal, q, pass_send, pass_recv, sibling).wait_recv()

        def columns(n, carry):
            cols = pl.ds(pl.multiple_of(n * tile, tile), tile)
            acc = None
            for s in range(4):
                term = jnp.dot(
                    attention[s, part(q), :],
                    weight[pl.ds(s * width, width), cols],
                    preferred_element_type=jnp.float32,
                )
                acc = term if acc is None else acc + term
            for i in range(part_rows // window):
                r = q * (part_rows // window) + i
                at = pl.ds(r * window, window)
                total[at, cols] = (
                    residual[at, cols].astype(jnp.float32)
                    + gate[pl.ds(r, 1), cols] * acc[i * window:(i + 1) * window]
                )
            return carry

        lax.fori_loop(0, width // tile, columns, 0)

    def sum_copy(step):
        to = lax.rem(t + step, 4)
        return pltpu.make_async_remote_copy(
            src_ref=partial.at[pl.ds(to * own_pairs, own_pairs)], dst_ref=arrived.at[step - 1],
            send_sem=sum_send.at[step - 1], recv_sem=sum_recv.at[step - 1],
            device_id={"tensor": to}, device_id_type=MESH,
        )

    def low_copy(step, owner):
        ref = low.at[pl.ds(owner * own_pairs, own_pairs)]
        return pltpu.make_async_remote_copy(
            src_ref=ref, dst_ref=ref,
            send_sem=low_send.at[step - 1], recv_sem=low_recv.at[step - 1],
            device_id={"tensor": lax.rem(t + step, 4)}, device_id_type=MESH,
        )

    def project_down():
        def one(r):
            x = attention[t, pl.ds(pl.multiple_of(r * window, window), window), :]
            return lax.dot_general(
                x, down[index[r]], (((1,), (1,)), ((), ())), preferred_element_type=jnp.float32
            )

        def pair(p, carry):
            partial[p] = jnp.concatenate([one(2 * p), one(2 * p + 1)], axis=1)
            return carry

        lax.fori_loop(0, pairs, pair, 0)

    start_own(0)
    for q in range(PARTS):
        across_copy(q).start()
        near_copy(q).start()
    gate[...] = gate_in[...].astype(jnp.float32)

    for j in range(PIECES):
        relay(0, 0, j)
    relay_attention(0)
    for j in range(PIECES):
        relay(0, 1, j)
    relay_attention(1)
    start_own(1)
    local[0].wait()
    local[2].wait()
    local[3].wait()
    base_part(0)
    for hop in range(2, hops):
        for j in range(PIECES):
            relay(0, hop, j)
    base_part(1)
    relay_attention(2)

    local[1].wait()
    await_other_group(0)
    project_down()
    for step in (1, 2, 3):
        sum_copy(step).start()
    for j in range(PIECES):
        relay(1, 0, j)
    for step in (1, 2, 3):
        sum_copy(step).wait_recv()
    own = pl.ds(t * own_pairs, own_pairs)
    low[own] = (partial[own] + arrived[0] + arrived[1] + arrived[2]).astype(jnp.bfloat16)
    for step in (1, 2, 3):
        low_copy(step, t).start()
    for j in range(PIECES):
        relay(1, 1, j)
    relay_attention(3)
    base_part(2)
    for hop in range(2, hops):
        for j in range(PIECES):
            relay(1, hop, j)
    base_part(3)

    for step in (1, 2, 3):
        low_copy(step, lax.rem(t + 4 - step, 4)).wait_recv()
    local[4].wait()
    await_other_group(1)
    writes = []
    for q in range(PARTS):
        def pair(p, carry):
            both = low[p]
            for i in (0, 1):
                r = 2 * p + i
                at = pl.ds(pl.multiple_of(r * window, window), window)
                delta = jnp.dot(
                    both[:, i * rank:(i + 1) * rank], up[index[r]], preferred_element_type=jnp.float32
                )
                result[at, :] = (total[at, :] + gate[pl.ds(r, 1), :] * delta).astype(result.dtype)
            return carry

        lax.fori_loop(q * pairs // PARTS, (q + 1) * pairs // PARTS, pair, 0)
        write = pltpu.make_async_copy(result.at[part(q)], out.at[part(q)], out_sem.at[q])
        write.start()
        writes.append(write)

    for stage in (0, 1):
        for hop in range(hops):
            for j in range(PIECES):
                for way in (0, 1):
                    @pl.when(sends(way, hop))
                    def _():
                        z_copy(stage, way, hop, j).wait_send()

                    @pl.when(receives(way, hop))
                    def _():
                        y_copy(stage, way, hop, j, g).wait_send()
    for q in range(PARTS):
        across_copy(q).wait_send()
        near_copy(q).wait_send()
        pass_copy(q).wait_send()
    for step in (1, 2, 3):
        sum_copy(step).wait_send()
        low_copy(step, t).wait_send()
    for write in writes:
        write.wait()


def fused_body(
    holders,
    residual,
    attention,
    gate,
    output_projection_weight,
    adapter_down_weight,
    adapter_up_weight,
    request_adapter_index,
):
    rows, width = attention.shape
    requests = gate.shape[0]
    share, rank, _ = adapter_down_weight.shape
    window = rows // requests
    pairs = requests // 2
    hops = holders - 1
    bf16, f32 = jnp.bfloat16, jnp.float32
    dma = pltpu.SemaphoreType.DMA
    z = 4 * hops * PIECES
    anywhere = pl.BlockSpec(memory_space=pl.ANY)
    return pl.pallas_call(
        functools.partial(fused_kernel, holders),
        out_shape=jax.ShapeDtypeStruct((rows, width), bf16),
        in_specs=[
            pl.BlockSpec(memory_space=pltpu.SMEM),
            pl.BlockSpec(memory_space=pltpu.VMEM),
            anywhere, anywhere, anywhere, anywhere, anywhere,
        ],
        out_specs=anywhere,
        scratch_shapes=[
            pltpu.VMEM((4, rows, width), bf16),
            pltpu.VMEM((4 * width, width), bf16),
            pltpu.VMEM((holders * share, rank, width), bf16),
            pltpu.VMEM((holders * share, rank, width), bf16),
            pltpu.VMEM((rows, width), bf16),
            pltpu.VMEM((requests, width), f32),
            pltpu.VMEM((rows, width), f32),
            pltpu.VMEM((rows, width), bf16),
            pltpu.VMEM((pairs, window, 2 * rank), f32),
            pltpu.VMEM((3, pairs // 4, window, 2 * rank), f32),
            pltpu.VMEM((pairs, window, 2 * rank), bf16),
            dma((z,)), dma((z,)), dma((z,)), dma((z,)),
            dma((PARTS,)), dma((PARTS,)), dma((PARTS,)), dma((PARTS,)), dma((PARTS,)), dma((PARTS,)),
            dma((3,)), dma((3,)), dma((3,)), dma((3,)),
            dma((5,)), dma((PARTS,)),
        ],
        compiler_params=pltpu.CompilerParams(
            collective_id=0, has_side_effects=True, vmem_limit_bytes=56 * 2**20
        ),
        cost_estimate=pl.CostEstimate(
            flops=2 * rows * width * (4 * width + 2 * rank), bytes_accessed=24 * 2**20, transcendentals=0
        ),
    )(
        request_adapter_index, gate, residual, attention,
        output_projection_weight, adapter_down_weight, adapter_up_weight,
    )


def solution(mesh):
    in_specs = (
        P(("groups", "dp"), "tensor"),
        P(("groups", "dp"), "tensor"),
        P(("groups", "dp"), "tensor"),
        P(None, "tensor"),
        P("dp", None, "tensor"),
        P("dp", None, "tensor"),
        P(("groups", "dp")),
    )
    out_specs = P(("groups", "dp"), "tensor")
    holders = mesh.shape["dp"]
    if mesh.shape["tensor"] == 4 and mesh.shape["groups"] == 2 and 2 < holders <= 8:
        body = functools.partial(fused_body, holders)
    else:
        body = exchange_body
    return jax.shard_map(body, mesh=mesh, in_specs=in_specs, out_specs=out_specs, check_vma=False)
```

```python
import functools

import jax
import jax.numpy as jnp
from jax import lax
from jax.experimental import pallas as pl
from jax.experimental.pallas import tpu as pltpu
from jax.sharding import PartitionSpec as P

MESH = pl.DeviceIdType.MESH
PIECES = 2
PARTS = 4


def exchange_body(
    residual,
    attention,
    gate,
    output_projection_weight,
    adapter_down_weight,
    adapter_up_weight,
    request_adapter_index,
):
    rows, width = attention.shape
    req_dev = request_adapter_index.shape[0]
    window = rows // req_dev
    holders = lax.axis_size("dp")
    adapter_device_share = adapter_down_weight.shape[0]
    capacity = max(1, 2 * req_dev // holders)
    total = holders * capacity
    owner = request_adapter_index // adapter_device_share
    local = request_adapter_index % adapter_device_share
    same_owner = owner[:, None] == owner[None, :]
    earlier = jnp.arange(req_dev)[None, :] < jnp.arange(req_dev)[:, None]
    place = jnp.sum(jnp.logical_and(same_owner, earlier).astype(jnp.int32), axis=1)
    target = owner * capacity + place
    onehot = jnp.arange(total)[:, None] == target[None, :]
    chosen = onehot.astype(jnp.bfloat16)
    flat = attention.reshape(req_dev, window * width)
    packed = jnp.dot(chosen, flat, preferred_element_type=jnp.float32).astype(jnp.bfloat16)
    packed = packed.reshape(holders, capacity, window, width)
    wanted = jnp.sum(onehot.astype(jnp.int32) * local[None, :], axis=1)
    wanted = wanted.reshape(holders, capacity)
    got_rows = lax.all_to_all(packed, "dp", split_axis=0, concat_axis=0, tiled=True)
    received_slots = lax.all_to_all(wanted, "dp", split_axis=0, concat_axis=0, tiled=True)
    down_matrix = jnp.take(adapter_down_weight, received_slots, axis=0)
    up_matrix = jnp.take(adapter_up_weight, received_slots, axis=0)
    partial_low = jnp.einsum(
        "ncwf,ncrf->ncwr", got_rows, down_matrix, preferred_element_type=jnp.float32
    )
    array_shape = partial_low.shape
    summed = lax.psum(
        partial_low.reshape(array_shape[0], array_shape[1], array_shape[2] * array_shape[3]),
        "tensor",
    )
    low = summed.reshape(array_shape).astype(jnp.bfloat16)
    delta = jnp.einsum(
        "ncwr,ncrf->ncwf", low, up_matrix, preferred_element_type=jnp.float32
    ).astype(jnp.bfloat16)
    returned = lax.all_to_all(delta, "dp", split_axis=0, concat_axis=0, tiled=True)
    gathered_back = jnp.dot(
        chosen.T, returned.reshape(total, window * width), preferred_element_type=jnp.float32
    )
    delta_rows = gathered_back.reshape(rows, width)
    base = jnp.dot(
        lax.all_gather(attention, "tensor", axis=1, tiled=True),
        output_projection_weight,
        preferred_element_type=jnp.float32,
    )
    scale = jnp.repeat(gate, window, axis=0).astype(jnp.float32)
    updated = residual.astype(jnp.float32) + scale * (base + delta_rows)
    return updated.astype(jnp.bfloat16)


def fused_kernel(
    holders,
    index,
    index_in,
    gate_in,
    residual_in,
    attention_in,
    weight_in,
    down_in,
    up_in,
    out,
    attention,
    weight,
    down,
    up,
    residual,
    gate,
    total,
    result,
    partial,
    arrived,
    low,
    guest,
    guest_index,
    help_out,
    help_in,
    z_send,
    z_recv,
    y_send,
    y_recv,
    x_send,
    x_recv,
    near_send,
    near_recv,
    pass_send,
    pass_recv,
    sum_send,
    sum_recv,
    low_send,
    low_recv,
    more_send,
    more_recv,
    guest_send,
    guest_recv,
    local_sem,
    out_sem,
):
    g = lax.axis_index("groups")
    d = lax.axis_index("dp")
    t = lax.axis_index("tensor")
    core = lax.rem(t, 2)
    sibling = t + 1 - 2 * core
    across = lax.rem(t + 2, 4)
    diagonal = lax.rem(sibling + 2, 4)

    rows, width = attention_in.shape
    requests = gate_in.shape[0]
    window = rows // requests
    share, rank, _ = down_in.shape
    half = share // 2
    piece = half // PIECES
    part_rows = rows // PARTS
    pairs = requests // 2
    own_pairs = pairs // 4
    hops = holders - 1
    inputs, buffers = (down_in, up_in), (down, up)
    at_end = jnp.logical_or(d == 0, d == holders - 1)
    inside = jnp.logical_not(at_end)
    partner = d + 1 - 2 * lax.rem(d, 2)
    first, last = pl.ds(0, width // 2), pl.ds(width // 2, width // 2)

    own_block = pl.ds(d * share, share)
    local = [
        pltpu.make_async_copy(src, dst, local_sem.at[i])
        for i, (src, dst) in enumerate(
            [
                (attention_in, attention.at[t]),
                (down_in, down.at[own_block]),
                (weight_in, weight),
                (residual_in, residual),
                (up_in, up.at[own_block]),
            ]
        )
    ]

    barrier = pltpu.get_barrier_semaphore()

    def greet(where):
        pl.semaphore_signal(barrier, inc=1, device_id=where, device_id_type=MESH)

    for step in (1, 2, 3):
        greet({"tensor": lax.rem(t + step, 4)})
    greet({"groups": 1 - g})

    @pl.when(d > 0)
    def _():
        greet({"dp": d - 1})

    @pl.when(d < holders - 1)
    def _():
        greet({"dp": d + 1})

    for copy in local:
        copy.start()
    pl.semaphore_wait(barrier, 4 + (d > 0).astype(jnp.int32) + (d < holders - 1).astype(jnp.int32))

    def slot(stage, way, hop, j):
        return ((stage * 2 + way) * hops + hop) * PIECES + j

    def place(holder, side, j):
        return pl.ds(holder * share + side * half + j * piece, piece)

    def rank_on(way):
        return d if way == 0 else holders - 1 - d

    def sends(way, hop):
        e = rank_on(way)
        return jnp.logical_and(e < holders - 1, e >= hop)

    def receives(way, hop):
        return rank_on(way) > hop

    def at_edge(way):
        return d == (holders - 2 if way == 0 else 1)

    def cut(ref, stage, narrow):
        return ref.at[:, :, last] if narrow else ref

    def either(stage, narrow, act):
        if stage == 1:
            act(False)
        else:
            pl.when(narrow)(lambda: act(True))
            pl.when(jnp.logical_not(narrow))(lambda: act(False))

    def z_copy(stage, way, hop, j, narrow):
        sign = 1 if way == 0 else -1
        target = buffers[stage].at[place(d - sign * hop, g, j)]
        source = inputs[stage].at[pl.ds(g * half + j * piece, piece)] if hop == 0 else target
        i = slot(stage, way, hop, j)
        return pltpu.make_async_remote_copy(
            src_ref=cut(source, stage, narrow), dst_ref=cut(target, stage, narrow),
            send_sem=z_send.at[i], recv_sem=z_recv.at[i],
            device_id={"dp": d + sign}, device_id_type=MESH,
        )

    def z_start(stage, way, hop, j):
        either(stage, at_edge(way), lambda n: z_copy(stage, way, hop, j, n).start())

    def z_sent(stage, way, hop, j):
        either(stage, at_edge(way), lambda n: z_copy(stage, way, hop, j, n).wait_send())

    def z_arrival(stage, way, hop, j, narrow):
        sign = 1 if way == 0 else -1
        target = cut(buffers[stage].at[place(d - sign * (hop + 1), g, j)], stage, narrow)
        i = slot(stage, way, hop, j)
        return pltpu.make_async_remote_copy(
            src_ref=target, dst_ref=target, send_sem=z_send.at[i], recv_sem=z_recv.at[i],
            device_id={"dp": d - sign}, device_id_type=MESH,
        )

    def y_copy(stage, way, hop, j, side, narrow):
        sign = 1 if way == 0 else -1
        target = cut(buffers[stage].at[place(d - sign * (hop + 1), side, j)], stage, narrow)
        i = slot(stage, way, hop, j)
        return pltpu.make_async_remote_copy(
            src_ref=target, dst_ref=target, send_sem=y_send.at[i], recv_sem=y_recv.at[i],
            device_id={"groups": 1 - g}, device_id_type=MESH,
        )

    def over_y(stage, way, hop, act):
        if stage == 1 and hop == 0:
            pl.when(jnp.logical_not(at_edge(way)))(lambda: act(False))
        else:
            either(stage, at_end, act)

    def more_copy(j, holder):
        target = up.at[place(holder, 1 - g, j)]
        return pltpu.make_async_remote_copy(
            src_ref=up_in.at[pl.ds((1 - g) * half + j * piece, piece)], dst_ref=target,
            send_sem=more_send.at[j], recv_sem=more_recv.at[j],
            device_id={"dp": holders - 1 - d}, device_id_type=MESH,
        )

    def start_own(stage):
        for j in range(PIECES):
            for way in (0, 1):
                @pl.when(sends(way, 0))
                def _():
                    z_start(stage, way, 0, j)
        if stage == 1:
            @pl.when(inside)
            def _():
                for j in range(PIECES):
                    more_copy(j, d).start()

    def relay(stage, hop, j):
        for way in (0, 1):
            @pl.when(receives(way, hop))
            def _():
                either(stage, at_end, lambda n: z_arrival(stage, way, hop, j, n).wait_recv())
                if hop + 1 < hops:
                    @pl.when(sends(way, hop + 1))
                    def _():
                        z_start(stage, way, hop + 1, j)
                over_y(stage, way, hop, lambda n: y_copy(stage, way, hop, j, g, n).start())

    def await_other_group(stage):
        for hop in range(hops):
            for j in range(PIECES):
                for way in (0, 1):
                    @pl.when(receives(way, hop))
                    def _():
                        over_y(stage, way, hop, lambda n: y_copy(stage, way, hop, j, 1 - g, n).wait_recv())
        if stage == 1:
            @pl.when(inside)
            def _():
                for j in range(PIECES):
                    more_copy(j, holders - 1 - d).wait_recv()

    def guest_copy(i):
        src, dst = [(index_in, guest_index), (attention_in.at[:, first], guest), (help_out, help_in)][i]
        return pltpu.make_async_remote_copy(
            src_ref=src, dst_ref=dst, send_sem=guest_send.at[i], recv_sem=guest_recv.at[i],
            device_id={"dp": partner}, device_id_type=MESH,
        )

    def part(q):
        return pl.ds(q * part_rows, part_rows)

    def attention_copy(source, which, q, send, recv, to):
        return pltpu.make_async_remote_copy(
            src_ref=source, dst_ref=attention.at[which, part(q)],
            send_sem=send.at[q], recv_sem=recv.at[q],
            device_id={"tensor": to}, device_id_type=MESH,
        )

    def across_copy(q):
        return attention_copy(attention_in.at[part(q)], t, q, x_send, x_recv, across)

    def near_copy(q):
        return attention_copy(attention_in.at[part(q)], t, q, near_send, near_recv, sibling)

    def pass_copy(q):
        return attention_copy(attention.at[across, part(q)], across, q, pass_send, pass_recv, sibling)

    def relay_attention(q):
        attention_copy(attention.at[across, part(q)], across, q, x_send, x_recv, across).wait_recv()
        pass_copy(q).start()

    tile = 256

    def base_part(q):
        attention_copy(attention.at[sibling, part(q)], sibling, q, near_send, near_recv, sibling).wait_recv()
        attention_copy(attention.at[diagonal, part(q)], diagonal, q, pass_send, pass_recv, sibling).wait_recv()

        def columns(n, carry):
            cols = pl.ds(pl.multiple_of(n * tile, tile), tile)
            acc = None
            for s in range(4):
                term = jnp.dot(
                    attention[s, part(q), :],
                    weight[pl.ds(s * width, width), cols],
                    preferred_element_type=jnp.float32,
                )
                acc = term if acc is None else acc + term
            for i in range(part_rows // window):
                r = q * (part_rows // window) + i
                at = pl.ds(r * window, window)
                total[at, cols] = (
                    residual[at, cols].astype(jnp.float32)
                    + gate[pl.ds(r, 1), cols] * acc[i * window:(i + 1) * window]
                )
            return carry

        lax.fori_loop(0, width // tile, columns, 0)

    def sum_copy(which, step):
        to = lax.rem(t + step, 4)
        return pltpu.make_async_remote_copy(
            src_ref=partial.at[which, pl.ds(to * own_pairs, own_pairs)], dst_ref=arrived.at[which, step - 1],
            send_sem=sum_send.at[which * 3 + step - 1], recv_sem=sum_recv.at[which * 3 + step - 1],
            device_id={"tensor": to}, device_id_type=MESH,
        )

    def low_copy(step, owner):
        ref = low.at[pl.ds(owner * own_pairs, own_pairs)]
        return pltpu.make_async_remote_copy(
            src_ref=ref, dst_ref=ref,
            send_sem=low_send.at[step - 1], recv_sem=low_recv.at[step - 1],
            device_id={"tensor": lax.rem(t + step, 4)}, device_id_type=MESH,
        )

    def project_down(which, rows_of, chosen, cols):
        def one(r):
            x = rows_of(pl.ds(pl.multiple_of(r * window, window), window))
            return lax.dot_general(
                x, down[chosen[r], :, cols], (((1,), (1,)), ((), ())), preferred_element_type=jnp.float32
            )

        def pair(p, carry):
            partial[which, p] = jnp.concatenate([one(2 * p), one(2 * p + 1)], axis=1)
            return carry

        lax.fori_loop(0, pairs, pair, 0)
        for step in (1, 2, 3):
            sum_copy(which, step).start()

    own = pl.ds(t * own_pairs, own_pairs)

    def summed(which):
        for step in (1, 2, 3):
            sum_copy(which, step).wait_recv()
        return partial[which, own] + arrived[which, 0] + arrived[which, 1] + arrived[which, 2]

    def share_low(value):
        low[own] = value.astype(jnp.bfloat16)
        for step in (1, 2, 3):
            low_copy(step, t).start()

    start_own(0)

    @pl.when(at_end)
    def _():
        guest_copy(0).start()
        guest_copy(1).start()

    for q in range(PARTS):
        across_copy(q).start()
        near_copy(q).start()
    gate[...] = gate_in[...].astype(jnp.float32)

    for j in range(PIECES):
        relay(0, 0, j)
    start_own(1)
    relay_attention(0)
    for j in range(PIECES):
        relay(0, 1, j)
    local[0].wait()
    local[2].wait()
    local[3].wait()
    base_part(0)
    for hop in range(2, hops):
        for j in range(PIECES):
            relay(0, hop, j)
    relay_attention(1)
    base_part(1)

    local[1].wait()
    await_other_group(0)

    @pl.when(at_end)
    def _():
        project_down(0, lambda at: attention[t, at, last], index, last)

    @pl.when(inside)
    def _():
        guest_copy(0).wait_recv()
        guest_copy(1).wait_recv()
        project_down(1, lambda at: guest[at, :], guest_index, first)
        project_down(0, lambda at: attention[t, at, :], index, pl.ds(0, width))

    for j in range(PIECES):
        relay(1, 0, j)
    relay_attention(2)

    @pl.when(inside)
    def _():
        help_out[...] = summed(1)
        guest_copy(2).start()
        share_low(summed(0))

    for j in range(PIECES):
        relay(1, 1, j)
    relay_attention(3)
    base_part(2)
    for hop in range(2, hops):
        for j in range(PIECES):
            relay(1, hop, j)

    @pl.when(at_end)
    def _():
        guest_copy(2).wait_recv()
        share_low(summed(0) + help_in[...])

    base_part(3)

    for step in (1, 2, 3):
        low_copy(step, lax.rem(t + 4 - step, 4)).wait_recv()
    local[4].wait()
    await_other_group(1)
    writes = []
    for q in range(PARTS):
        def pair(p, carry):
            both = low[p]
            for i in (0, 1):
                r = 2 * p + i
                at = pl.ds(pl.multiple_of(r * window, window), window)
                delta = jnp.dot(
                    both[:, i * rank:(i + 1) * rank], up[index[r]], preferred_element_type=jnp.float32
                )
                result[at, :] = (total[at, :] + gate[pl.ds(r, 1), :] * delta).astype(result.dtype)
            return carry

        lax.fori_loop(q * pairs // PARTS, (q + 1) * pairs // PARTS, pair, 0)
        write = pltpu.make_async_copy(result.at[part(q)], out.at[part(q)], out_sem.at[q])
        write.start()
        writes.append(write)

    for stage in (0, 1):
        for hop in range(hops):
            for j in range(PIECES):
                for way in (0, 1):
                    @pl.when(sends(way, hop))
                    def _():
                        z_sent(stage, way, hop, j)

                    @pl.when(receives(way, hop))
                    def _():
                        over_y(stage, way, hop, lambda n: y_copy(stage, way, hop, j, g, n).wait_send())
    for q in range(PARTS):
        across_copy(q).wait_send()
        near_copy(q).wait_send()
        pass_copy(q).wait_send()
    for step in (1, 2, 3):
        sum_copy(0, step).wait_send()
        low_copy(step, t).wait_send()

    @pl.when(at_end)
    def _():
        guest_copy(0).wait_send()
        guest_copy(1).wait_send()

    @pl.when(inside)
    def _():
        guest_copy(2).wait_send()
        for step in (1, 2, 3):
            sum_copy(1, step).wait_send()
        for j in range(PIECES):
            more_copy(j, d).wait_send()

    for write in writes:
        write.wait()


def fused_body(
    holders,
    residual,
    attention,
    gate,
    output_projection_weight,
    adapter_down_weight,
    adapter_up_weight,
    request_adapter_index,
):
    rows, width = attention.shape
    requests = gate.shape[0]
    share, rank, _ = adapter_down_weight.shape
    window = rows // requests
    pairs = requests // 2
    hops = holders - 1
    bf16, f32 = jnp.bfloat16, jnp.float32
    dma = pltpu.SemaphoreType.DMA
    z = 4 * hops * PIECES
    anywhere = pl.BlockSpec(memory_space=pl.ANY)
    return pl.pallas_call(
        functools.partial(fused_kernel, holders),
        out_shape=jax.ShapeDtypeStruct((rows, width), bf16),
        in_specs=[
            pl.BlockSpec(memory_space=pltpu.SMEM),
            anywhere,
            pl.BlockSpec(memory_space=pltpu.VMEM),
            anywhere, anywhere, anywhere, anywhere, anywhere,
        ],
        out_specs=anywhere,
        scratch_shapes=[
            pltpu.VMEM((4, rows, width), bf16),
            pltpu.VMEM((4 * width, width), bf16),
            pltpu.VMEM((holders * share, rank, width), bf16),
            pltpu.VMEM((holders * share, rank, width), bf16),
            pltpu.VMEM((rows, width), bf16),
            pltpu.VMEM((requests, width), f32),
            pltpu.VMEM((rows, width), f32),
            pltpu.VMEM((rows, width), bf16),
            pltpu.VMEM((2, pairs, window, 2 * rank), f32),
            pltpu.VMEM((2, 3, pairs // 4, window, 2 * rank), f32),
            pltpu.VMEM((pairs, window, 2 * rank), bf16),
            pltpu.VMEM((rows, width // 2), bf16),
            pltpu.SMEM((requests,), jnp.int32),
            pltpu.VMEM((pairs // 4, window, 2 * rank), f32),
            pltpu.VMEM((pairs // 4, window, 2 * rank), f32),
            dma((z,)), dma((z,)), dma((z,)), dma((z,)),
            dma((PARTS,)), dma((PARTS,)), dma((PARTS,)), dma((PARTS,)), dma((PARTS,)), dma((PARTS,)),
            dma((6,)), dma((6,)), dma((3,)), dma((3,)),
            dma((PIECES,)), dma((PIECES,)), dma((3,)), dma((3,)),
            dma((5,)), dma((PARTS,)),
        ],
        compiler_params=pltpu.CompilerParams(
            collective_id=0, has_side_effects=True, vmem_limit_bytes=56 * 2**20
        ),
        cost_estimate=pl.CostEstimate(
            flops=2 * rows * width * (4 * width + 2 * rank), bytes_accessed=24 * 2**20, transcendentals=0
        ),
    )(
        request_adapter_index, request_adapter_index, gate, residual, attention,
        output_projection_weight, adapter_down_weight, adapter_up_weight,
    )


def solution(mesh):
    in_specs = (
        P(("groups", "dp"), "tensor"),
        P(("groups", "dp"), "tensor"),
        P(("groups", "dp"), "tensor"),
        P(None, "tensor"),
        P("dp", None, "tensor"),
        P("dp", None, "tensor"),
        P(("groups", "dp")),
    )
    out_specs = P(("groups", "dp"), "tensor")
    holders = mesh.shape["dp"]
    if mesh.shape["tensor"] == 4 and mesh.shape["groups"] == 2 and holders == 4:
        body = functools.partial(fused_body, holders)
    else:
        body = exchange_body
    return jax.shard_map(body, mesh=mesh, in_specs=in_specs, out_specs=out_specs, check_vma=False)
```

```python
import functools

import jax
import jax.numpy as jnp
from jax import lax
from jax.experimental import pallas as pl
from jax.experimental.pallas import tpu as pltpu
from jax.sharding import PartitionSpec as P

MESH = pl.DeviceIdType.MESH
PIECES = 4
PARTS = 4


def exchange_body(
    residual,
    attention,
    gate,
    output_projection_weight,
    adapter_down_weight,
    adapter_up_weight,
    request_adapter_index,
):
    rows, width = attention.shape
    req_dev = request_adapter_index.shape[0]
    window = rows // req_dev
    holders = lax.axis_size("dp")
    adapter_device_share = adapter_down_weight.shape[0]
    capacity = max(1, 2 * req_dev // holders)
    total = holders * capacity
    owner = request_adapter_index // adapter_device_share
    local = request_adapter_index % adapter_device_share
    same_owner = owner[:, None] == owner[None, :]
    earlier = jnp.arange(req_dev)[None, :] < jnp.arange(req_dev)[:, None]
    place = jnp.sum(jnp.logical_and(same_owner, earlier).astype(jnp.int32), axis=1)
    target = owner * capacity + place
    onehot = jnp.arange(total)[:, None] == target[None, :]
    chosen = onehot.astype(jnp.bfloat16)
    flat = attention.reshape(req_dev, window * width)
    packed = jnp.dot(chosen, flat, preferred_element_type=jnp.float32).astype(jnp.bfloat16)
    packed = packed.reshape(holders, capacity, window, width)
    wanted = jnp.sum(onehot.astype(jnp.int32) * local[None, :], axis=1)
    wanted = wanted.reshape(holders, capacity)
    got_rows = lax.all_to_all(packed, "dp", split_axis=0, concat_axis=0, tiled=True)
    received_slots = lax.all_to_all(wanted, "dp", split_axis=0, concat_axis=0, tiled=True)
    down_matrix = jnp.take(adapter_down_weight, received_slots, axis=0)
    up_matrix = jnp.take(adapter_up_weight, received_slots, axis=0)
    partial_low = jnp.einsum(
        "ncwf,ncrf->ncwr", got_rows, down_matrix, preferred_element_type=jnp.float32
    )
    array_shape = partial_low.shape
    summed = lax.psum(
        partial_low.reshape(array_shape[0], array_shape[1], array_shape[2] * array_shape[3]),
        "tensor",
    )
    low = summed.reshape(array_shape).astype(jnp.bfloat16)
    delta = jnp.einsum(
        "ncwr,ncrf->ncwf", low, up_matrix, preferred_element_type=jnp.float32
    ).astype(jnp.bfloat16)
    returned = lax.all_to_all(delta, "dp", split_axis=0, concat_axis=0, tiled=True)
    gathered_back = jnp.dot(
        chosen.T, returned.reshape(total, window * width), preferred_element_type=jnp.float32
    )
    delta_rows = gathered_back.reshape(rows, width)
    base = jnp.dot(
        lax.all_gather(attention, "tensor", axis=1, tiled=True),
        output_projection_weight,
        preferred_element_type=jnp.float32,
    )
    scale = jnp.repeat(gate, window, axis=0).astype(jnp.float32)
    updated = residual.astype(jnp.float32) + scale * (base + delta_rows)
    return updated.astype(jnp.bfloat16)


def fused_kernel(
    holders,
    index,
    index_in,
    gate_in,
    residual_in,
    attention_in,
    weight_in,
    down_in,
    up_in,
    out,
    attention,
    weight,
    down,
    up,
    residual,
    gate,
    total,
    result,
    partial,
    arrived,
    low,
    guest,
    guest_index,
    help_out,
    help_in,
    z_send,
    z_recv,
    y_send,
    y_recv,
    x_send,
    x_recv,
    near_send,
    near_recv,
    pass_send,
    pass_recv,
    sum_send,
    sum_recv,
    low_send,
    low_recv,
    more_send,
    more_recv,
    guest_send,
    guest_recv,
    local_sem,
    out_sem,
):
    g = lax.axis_index("groups")
    d = lax.axis_index("dp")
    t = lax.axis_index("tensor")
    core = lax.rem(t, 2)
    sibling = t + 1 - 2 * core
    across = lax.rem(t + 2, 4)
    diagonal = lax.rem(sibling + 2, 4)

    rows, width = attention_in.shape
    requests = gate_in.shape[0]
    window = rows // requests
    share, rank, _ = down_in.shape
    half = share // 2
    piece = half // PIECES
    part_rows = rows // PARTS
    pairs = requests // 2
    own_pairs = pairs // 4
    hops = holders - 1
    inputs, buffers = (down_in, up_in), (down, up)
    at_end = jnp.logical_or(d == 0, d == holders - 1)
    inside = jnp.logical_not(at_end)
    partner = d + 1 - 2 * lax.rem(d, 2)
    first, last = pl.ds(0, width // 2), pl.ds(width // 2, width // 2)

    own_block = pl.ds(d * share, share)
    local = [
        pltpu.make_async_copy(src, dst, local_sem.at[i])
        for i, (src, dst) in enumerate(
            [
                (attention_in, attention.at[t]),
                (down_in, down.at[own_block]),
                (weight_in, weight),
                (residual_in, residual),
                (up_in, up.at[own_block]),
            ]
        )
    ]

    barrier = pltpu.get_barrier_semaphore()

    def greet(where):
        pl.semaphore_signal(barrier, inc=1, device_id=where, device_id_type=MESH)

    for step in (1, 2, 3):
        greet({"tensor": lax.rem(t + step, 4)})
    greet({"groups": 1 - g})

    @pl.when(d > 0)
    def _():
        greet({"dp": d - 1})

    @pl.when(d < holders - 1)
    def _():
        greet({"dp": d + 1})

    for copy in local:
        copy.start()
    pl.semaphore_wait(barrier, 4 + (d > 0).astype(jnp.int32) + (d < holders - 1).astype(jnp.int32))

    def slot(stage, way, hop, j):
        return ((stage * 2 + way) * hops + hop) * PIECES + j

    def place(holder, side, j):
        return pl.ds(holder * share + side * half + j * piece, piece)

    def rank_on(way):
        return d if way == 0 else holders - 1 - d

    def sends(way, hop):
        e = rank_on(way)
        return jnp.logical_and(e < holders - 1, e >= hop)

    def receives(way, hop):
        return rank_on(way) > hop

    def at_edge(way):
        return d == (holders - 2 if way == 0 else 1)

    def cut(ref, stage, narrow):
        return ref.at[:, :, last] if narrow else ref

    def either(stage, narrow, act):
        if stage == 1:
            act(False)
        else:
            pl.when(narrow)(lambda: act(True))
            pl.when(jnp.logical_not(narrow))(lambda: act(False))

    def z_copy(stage, way, hop, j, narrow):
        sign = 1 if way == 0 else -1
        target = buffers[stage].at[place(d - sign * hop, g, j)]
        source = inputs[stage].at[pl.ds(g * half + j * piece, piece)] if hop == 0 else target
        i = slot(stage, way, hop, j)
        return pltpu.make_async_remote_copy(
            src_ref=cut(source, stage, narrow), dst_ref=cut(target, stage, narrow),
            send_sem=z_send.at[i], recv_sem=z_recv.at[i],
            device_id={"dp": d + sign}, device_id_type=MESH,
        )

    def z_start(stage, way, hop, j):
        either(stage, at_edge(way), lambda n: z_copy(stage, way, hop, j, n).start())

    def z_sent(stage, way, hop, j):
        either(stage, at_edge(way), lambda n: z_copy(stage, way, hop, j, n).wait_send())

    def z_arrival(stage, way, hop, j, narrow):
        sign = 1 if way == 0 else -1
        target = cut(buffers[stage].at[place(d - sign * (hop + 1), g, j)], stage, narrow)
        i = slot(stage, way, hop, j)
        return pltpu.make_async_remote_copy(
            src_ref=target, dst_ref=target, send_sem=z_send.at[i], recv_sem=z_recv.at[i],
            device_id={"dp": d - sign}, device_id_type=MESH,
        )

    def y_copy(stage, way, hop, j, side, narrow):
        sign = 1 if way == 0 else -1
        target = cut(buffers[stage].at[place(d - sign * (hop + 1), side, j)], stage, narrow)
        i = slot(stage, way, hop, j)
        return pltpu.make_async_remote_copy(
            src_ref=target, dst_ref=target, send_sem=y_send.at[i], recv_sem=y_recv.at[i],
            device_id={"groups": 1 - g}, device_id_type=MESH,
        )

    def over_y(stage, way, hop, act):
        if stage == 1 and hop == 0:
            pl.when(jnp.logical_not(at_edge(way)))(lambda: act(False))
        else:
            either(stage, at_end, act)

    def more_copy(j, holder):
        target = up.at[place(holder, 1 - g, j)]
        return pltpu.make_async_remote_copy(
            src_ref=up_in.at[pl.ds((1 - g) * half + j * piece, piece)], dst_ref=target,
            send_sem=more_send.at[j], recv_sem=more_recv.at[j],
            device_id={"dp": holders - 1 - d}, device_id_type=MESH,
        )

    def start_own(stage):
        for j in range(PIECES):
            for way in (0, 1):
                @pl.when(sends(way, 0))
                def _():
                    z_start(stage, way, 0, j)

    def relay(stage, hop, j, also=lambda way: True):
        for way in (0, 1):
            @pl.when(jnp.logical_and(receives(way, hop), also(way)))
            def _():
                either(stage, at_end, lambda n: z_arrival(stage, way, hop, j, n).wait_recv())
                if hop + 1 < hops:
                    @pl.when(sends(way, hop + 1))
                    def _():
                        z_start(stage, way, hop + 1, j)
                over_y(stage, way, hop, lambda n: y_copy(stage, way, hop, j, g, n).start())

    def await_other_group(stage):
        for hop in range(hops):
            for j in range(PIECES):
                for way in (0, 1):
                    @pl.when(receives(way, hop))
                    def _():
                        over_y(stage, way, hop, lambda n: y_copy(stage, way, hop, j, 1 - g, n).wait_recv())
        if stage == 1:
            @pl.when(inside)
            def _():
                for j in range(PIECES):
                    more_copy(j, holders - 1 - d).wait_recv()

    def guest_copy(i):
        src, dst = [(index_in, guest_index), (attention_in.at[:, first], guest), (help_out, help_in)][i]
        return pltpu.make_async_remote_copy(
            src_ref=src, dst_ref=dst, send_sem=guest_send.at[i], recv_sem=guest_recv.at[i],
            device_id={"dp": partner}, device_id_type=MESH,
        )

    def part(q):
        return pl.ds(q * part_rows, part_rows)

    def attention_copy(source, which, q, send, recv, to):
        return pltpu.make_async_remote_copy(
            src_ref=source, dst_ref=attention.at[which, part(q)],
            send_sem=send.at[q], recv_sem=recv.at[q],
            device_id={"tensor": to}, device_id_type=MESH,
        )

    def across_copy(q):
        return attention_copy(attention_in.at[part(q)], t, q, x_send, x_recv, across)

    def near_copy(q):
        return attention_copy(attention_in.at[part(q)], t, q, near_send, near_recv, sibling)

    def pass_copy(q):
        return attention_copy(attention.at[across, part(q)], across, q, pass_send, pass_recv, sibling)

    def relay_attention(q):
        attention_copy(attention.at[across, part(q)], across, q, x_send, x_recv, across).wait_recv()
        pass_copy(q).start()

    tile = 256

    def base_part(q):
        attention_copy(attention.at[sibling, part(q)], sibling, q, near_send, near_recv, sibling).wait_recv()
        attention_copy(attention.at[diagonal, part(q)], diagonal, q, pass_send, pass_recv, sibling).wait_recv()

        def columns(n, carry):
            cols = pl.ds(pl.multiple_of(n * tile, tile), tile)
            acc = None
            for s in range(4):
                term = jnp.dot(
                    attention[s, part(q), :],
                    weight[pl.ds(s * width, width), cols],
                    preferred_element_type=jnp.float32,
                )
                acc = term if acc is None else acc + term
            for i in range(part_rows // window):
                r = q * (part_rows // window) + i
                at = pl.ds(r * window, window)
                total[at, cols] = (
                    residual[at, cols].astype(jnp.float32)
                    + gate[pl.ds(r, 1), cols] * acc[i * window:(i + 1) * window]
                )
            return carry

        lax.fori_loop(0, width // tile, columns, 0)

    def sum_copy(which, step):
        to = lax.rem(t + step, 4)
        return pltpu.make_async_remote_copy(
            src_ref=partial.at[which, pl.ds(to * own_pairs, own_pairs)], dst_ref=arrived.at[which, step - 1],
            send_sem=sum_send.at[which * 3 + step - 1], recv_sem=sum_recv.at[which * 3 + step - 1],
            device_id={"tensor": to}, device_id_type=MESH,
        )

    def low_copy(step, owner):
        ref = low.at[pl.ds(owner * own_pairs, own_pairs)]
        return pltpu.make_async_remote_copy(
            src_ref=ref, dst_ref=ref,
            send_sem=low_send.at[step - 1], recv_sem=low_recv.at[step - 1],
            device_id={"tensor": lax.rem(t + step, 4)}, device_id_type=MESH,
        )

    def project_down(which, rows_of, chosen, cols):
        def one(r):
            x = rows_of(pl.ds(pl.multiple_of(r * window, window), window))
            return lax.dot_general(
                x, down[chosen[r], :, cols], (((1,), (1,)), ((), ())), preferred_element_type=jnp.float32
            )

        def pair(p, carry):
            partial[which, p] = jnp.concatenate([one(2 * p), one(2 * p + 1)], axis=1)
            return carry

        lax.fori_loop(0, pairs, pair, 0, unroll=4)
        for step in (1, 2, 3):
            sum_copy(which, step).start()

    own = pl.ds(t * own_pairs, own_pairs)

    def summed(which):
        for step in (1, 2, 3):
            sum_copy(which, step).wait_recv()
        return partial[which, own] + arrived[which, 0] + arrived[which, 1] + arrived[which, 2]

    def share_low(value):
        low[own] = value.astype(jnp.bfloat16)
        for step in (1, 2, 3):
            low_copy(step, t).start()

    start_own(0)

    @pl.when(at_end)
    def _():
        guest_copy(0).start()
        guest_copy(1).start()

    for q in range(PARTS):
        across_copy(q).start()
        near_copy(q).start()
    gate[...] = gate_in[...].astype(jnp.float32)

    for j in range(PIECES):
        relay(0, 0, j)
    relay_attention(0)
    for j in range(PIECES):
        relay(0, 1, j)
    start_own(1)
    relay_attention(1)
    local[0].wait()
    local[2].wait()
    local[3].wait()

    @pl.when(at_end)
    def _():
        for j in range(PIECES):
            relay(1, 0, j)
        for j in range(PIECES):
            relay(0, 2, j)

    base_part(0)
    base_part(1)

    @pl.when(inside)
    def _():
        for j in range(PIECES):
            relay(1, 0, j, at_edge)
        for j in range(PIECES):
            more_copy(j, d).start()

    local[1].wait()
    await_other_group(0)
    relay_attention(2)

    @pl.when(at_end)
    def _():
        project_down(0, lambda at: attention[t, at, last], index, last)
        for j in range(PIECES):
            relay(1, 1, j)

    @pl.when(inside)
    def _():
        guest_copy(0).wait_recv()
        guest_copy(1).wait_recv()
        project_down(1, lambda at: guest[at, :], guest_index, first)
        project_down(0, lambda at: attention[t, at, :], index, pl.ds(0, width))
        relay(1, 0, 0, lambda way: jnp.logical_not(at_edge(way)))
        help_out[...] = summed(1)
        guest_copy(2).start()
        for j in range(1, PIECES):
            relay(1, 0, j, lambda way: jnp.logical_not(at_edge(way)))
        share_low(summed(0))

    relay_attention(3)
    base_part(2)

    @pl.when(inside)
    def _():
        for j in range(PIECES):
            relay(1, 1, j)

    @pl.when(at_end)
    def _():
        for j in range(PIECES):
            relay(1, 2, j)
        guest_copy(2).wait_recv()
        share_low(summed(0) + help_in[...])

    base_part(3)

    for step in (1, 2, 3):
        low_copy(step, lax.rem(t + 4 - step, 4)).wait_recv()
    local[4].wait()
    await_other_group(1)
    writes = []
    for q in range(PARTS):
        def pair(p, carry):
            both = low[p]
            for i in (0, 1):
                r = 2 * p + i
                at = pl.ds(pl.multiple_of(r * window, window), window)
                delta = jnp.dot(
                    both[:, i * rank:(i + 1) * rank], up[index[r]], preferred_element_type=jnp.float32
                )
                result[at, :] = (total[at, :] + gate[pl.ds(r, 1), :] * delta).astype(result.dtype)
            return carry

        lax.fori_loop(q * pairs // PARTS, (q + 1) * pairs // PARTS, pair, 0, unroll=True)
        write = pltpu.make_async_copy(result.at[part(q)], out.at[part(q)], out_sem.at[q])
        write.start()
        writes.append(write)

    for stage in (0, 1):
        for hop in range(hops):
            for j in range(PIECES):
                for way in (0, 1):
                    @pl.when(sends(way, hop))
                    def _():
                        z_sent(stage, way, hop, j)

                    @pl.when(receives(way, hop))
                    def _():
                        over_y(stage, way, hop, lambda n: y_copy(stage, way, hop, j, g, n).wait_send())
    for q in range(PARTS):
        across_copy(q).wait_send()
        near_copy(q).wait_send()
        pass_copy(q).wait_send()
    for step in (1, 2, 3):
        sum_copy(0, step).wait_send()
        low_copy(step, t).wait_send()

    @pl.when(at_end)
    def _():
        guest_copy(0).wait_send()
        guest_copy(1).wait_send()

    @pl.when(inside)
    def _():
        guest_copy(2).wait_send()
        for step in (1, 2, 3):
            sum_copy(1, step).wait_send()
        for j in range(PIECES):
            more_copy(j, d).wait_send()

    for write in writes:
        write.wait()


def fused_body(
    holders,
    residual,
    attention,
    gate,
    output_projection_weight,
    adapter_down_weight,
    adapter_up_weight,
    request_adapter_index,
):
    rows, width = attention.shape
    requests = gate.shape[0]
    share, rank, _ = adapter_down_weight.shape
    window = rows // requests
    pairs = requests // 2
    hops = holders - 1
    bf16, f32 = jnp.bfloat16, jnp.float32
    dma = pltpu.SemaphoreType.DMA
    z = 4 * hops * PIECES
    anywhere = pl.BlockSpec(memory_space=pl.ANY)
    return pl.pallas_call(
        functools.partial(fused_kernel, holders),
        out_shape=jax.ShapeDtypeStruct((rows, width), bf16),
        in_specs=[
            pl.BlockSpec(memory_space=pltpu.SMEM),
            anywhere,
            pl.BlockSpec(memory_space=pltpu.VMEM),
            anywhere, anywhere, anywhere, anywhere, anywhere,
        ],
        out_specs=anywhere,
        scratch_shapes=[
            pltpu.VMEM((4, rows, width), bf16),
            pltpu.VMEM((4 * width, width), bf16),
            pltpu.VMEM((holders * share, rank, width), bf16),
            pltpu.VMEM((holders * share, rank, width), bf16),
            pltpu.VMEM((rows, width), bf16),
            pltpu.VMEM((requests, width), f32),
            pltpu.VMEM((rows, width), f32),
            pltpu.VMEM((rows, width), bf16),
            pltpu.VMEM((2, pairs, window, 2 * rank), f32),
            pltpu.VMEM((2, 3, pairs // 4, window, 2 * rank), f32),
            pltpu.VMEM((pairs, window, 2 * rank), bf16),
            pltpu.VMEM((rows, width // 2), bf16),
            pltpu.SMEM((requests,), jnp.int32),
            pltpu.VMEM((pairs // 4, window, 2 * rank), f32),
            pltpu.VMEM((pairs // 4, window, 2 * rank), f32),
            dma((z,)), dma((z,)), dma((z,)), dma((z,)),
            dma((PARTS,)), dma((PARTS,)), dma((PARTS,)), dma((PARTS,)), dma((PARTS,)), dma((PARTS,)),
            dma((6,)), dma((6,)), dma((3,)), dma((3,)),
            dma((PIECES,)), dma((PIECES,)), dma((3,)), dma((3,)),
            dma((5,)), dma((PARTS,)),
        ],
        compiler_params=pltpu.CompilerParams(
            collective_id=0, has_side_effects=True, vmem_limit_bytes=56 * 2**20
        ),
        cost_estimate=pl.CostEstimate(
            flops=2 * rows * width * (4 * width + 2 * rank), bytes_accessed=24 * 2**20, transcendentals=0
        ),
    )(
        request_adapter_index, request_adapter_index, gate, residual, attention,
        output_projection_weight, adapter_down_weight, adapter_up_weight,
    )


def solution(mesh):
    in_specs = (
        P(("groups", "dp"), "tensor"),
        P(("groups", "dp"), "tensor"),
        P(("groups", "dp"), "tensor"),
        P(None, "tensor"),
        P("dp", None, "tensor"),
        P("dp", None, "tensor"),
        P(("groups", "dp")),
    )
    out_specs = P(("groups", "dp"), "tensor")
    holders = mesh.shape["dp"]
    if mesh.shape["tensor"] == 4 and mesh.shape["groups"] == 2 and holders == 4:
        body = functools.partial(fused_body, holders)
    else:
        body = exchange_body
    return jax.shard_map(body, mesh=mesh, in_specs=in_specs, out_specs=out_specs, check_vma=False)
```
